1024 devices in a mesh: row: 16 (over x, z_hi), col: 64 (over z_lo, y, core).
Axes of the slice: x: 4, y: 8, z: 16 (z_hi: 4, z_lo: 4; z = z_hi * 4 + z_lo), core: 2. Of those that a mesh axis runs over, the one named last changes fastest.
Arguments:
- queries: bfloat16 [16384, 4096], P('row'), may hold values from -32 to 32
- positives: int32 [16384], P('row'), may hold values from 0 to 8191
- hard_blocks: int32 [32, 7], P('row'), may hold values from 0 to 63, all different within a row
- passages: bfloat16 [64, 128, 4096], P(None, 'row', 'col'), may hold values from -6 to 6
- hard_passages: bfloat16 [64, 64, 4096], P(None, 'row', 'col'), may hold values from -12 to 12
Outputs:
- losses: float32 [16384], P('row')
- passage_grads: bfloat16 [64, 128, 4096], P('col', 'row')
- hard_grads: bfloat16 [64, 64, 4096], P('col', 'row')
The draws below stay inside these ranges and needn't reach their ends.
Inputs may be any that keep to these rules, and one draw needn't show every extreme that they name: Each row of hard_blocks names 7 different hard blocks; every hard block is named by some query block.
All inputs are finite; a program needn't handle non-finite values.
Results may differ from the reference program's by a relative error of at most 0.017.
Values may be sent and summed in bfloat16 or wider, within the bound.
No kernel may reach another device: no remote copies, remote signals or barrier semaphores. Data moves between devices by JAX's collectives and lax.ppermute only.
A program may use at most 64 MiB of HBM per device.

```python
import math
import jax
import jax.numpy as jnp
from jax import lax

D = 4096
QB = 512
QBD = 2
PPD = 128
HR = 64
KH = 7
NQ = 16384
NQB = 32
NPOS = 8192
N_ROW = 16
N_COL = 64


aligned_rows = 4


ladder = (120.0, 180.0, 250.0, 330.0)


passage_level = 2.0


def drawn_picks(key):
    query_picks = jax.random.permutation(jax.random.fold_in(key, 101), NQ)[:aligned_rows].astype(jnp.int32)
    passage_picks = jax.random.permutation(jax.random.fold_in(key, 102), NPOS)[:2 * aligned_rows].astype(jnp.int32)
    return (query_picks, passage_picks)


def drawn_signs(key):
    first_signs = (jax.random.randint(jax.random.fold_in(key, 103), (aligned_rows, D), 0, 2, dtype=jnp.int32) * 2 - 1).astype(jnp.float32)
    halves = (jax.random.randint(jax.random.fold_in(key, 104), (aligned_rows, D // 2), 0, 2, dtype=jnp.int32) * 2 - 1).astype(jnp.float32)
    second_signs = first_signs * jnp.concatenate([halves, -halves], axis=1)
    jitter = jax.random.uniform(jax.random.fold_in(key, 105), (aligned_rows,), jnp.float32, -0.08, 0.08)
    strengths = jnp.array(ladder, jnp.float32) * jnp.exp(jitter)
    spacing = jax.random.uniform(jax.random.fold_in(key, 106), (aligned_rows,), jnp.float32, 1.2, 2.8)
    return (first_signs, second_signs, strengths, spacing)


def draw_queries(key, part):
    query_picks = drawn_picks(key)[0]
    first_signs, second_signs, strengths, spacing = drawn_signs(key)
    key = jax.random.fold_in(key, 11)
    background = jnp.clip(jax.random.normal(key, (NQ, D), jnp.float32), -6.0, 6.0)
    root = math.sqrt(D)
    leading = strengths / (passage_level * root)
    trailing = (strengths - spacing) / (passage_level * root)
    aligned = leading[:, None] * first_signs + trailing[:, None] * second_signs
    return background.at[query_picks].set(aligned).astype(jnp.bfloat16)


def draw_passages(key, part):
    passage_picks = drawn_picks(key)[1]
    first_signs, second_signs, strengths, spacing = drawn_signs(key)
    key = jax.random.fold_in(key, 12)
    background = jnp.clip(jax.random.normal(key, (NPOS, D), jnp.float32), -6.0, 6.0)
    aligned = passage_level * jnp.concatenate([first_signs, second_signs], axis=0)
    filled = background.at[passage_picks].set(aligned)
    return filled.reshape(N_COL, PPD, D).astype(jnp.bfloat16)


def draw_positives(key, part):
    query_picks, passage_picks = drawn_picks(key)
    key = jax.random.fold_in(key, 13)
    drawn = jax.random.randint(key, (NQ,), 0, NPOS, dtype=jnp.int32)
    return drawn.at[query_picks].set(passage_picks[:aligned_rows])


def block_levels(key, dims, split, smallest, top_value):
    factor_of, own = 1.0, jax.random.fold_in(key, 6)
    for axis_at, blocks in split:
        heights = jnp.exp(jax.random.uniform(jax.random.fold_in(own, axis_at), (blocks,), jnp.float32, smallest / len(split), top_value / len(split)))
        factor_of = factor_of * jnp.repeat(heights, dims[axis_at] // blocks).reshape([-1 if axis == axis_at else 1 for axis in range(len(dims))])
    return factor_of


def different_ones(rng, rows, count, top, lift):
    sequence = jax.random.permutation(jax.random.fold_in(rng, 1), count)
    favour = sequence
    for power in range(3):
        favour = favour * favour // count
    favour = favour * lift // count
    tickets = jax.random.randint(jax.random.fold_in(rng, 2), (rows, count), 0, 4096) + favour
    fixed_rows = jax.random.permutation(jax.random.fold_in(rng, 3), rows)[jnp.arange(count) % rows]
    tickets = jnp.where(jnp.arange(rows)[:, None] == fixed_rows[None, :], 1 << 14, tickets)
    score = tickets * count + jnp.arange(count)
    return lax.top_k(score.astype(jnp.int32), top)[1].astype(jnp.int32)


def noise(own_key, dims, deviation, limit, pieces=(), kind=jnp.bfloat16):
    result = jax.random.normal(own_key, dims, jnp.float32) * deviation
    if len(pieces) > 0:
        result = block_levels(own_key, dims, pieces, -0.22, 0.18) * result
    return jnp.clip(result, min=-limit, max=limit).astype(kind)


def setup_inputs(seed: int = 0) -> dict:
    streams_of = jax.random.split(jax.random.key(seed), 6)
    queries = draw_queries(jax.random.fold_in(streams_of[5], 71), 0)
    positives = draw_positives(jax.random.fold_in(streams_of[5], 71), 0)
    hard_blocks = different_ones(streams_of[2], NQB, N_COL, KH, 1792)
    passages = draw_passages(jax.random.fold_in(streams_of[5], 71), 0)
    hard_passages = noise(streams_of[4], (N_COL, HR, D), 2.0, 12.0, ((1, 16), (2, 64)))
    return {"queries": queries, "positives": positives, "hard_blocks": hard_blocks, "passages": passages, "hard_passages": hard_passages}


def reference(queries, positives, hard_blocks, passages, hard_passages):
    scale = D ** -0.5
    rows_per = QBD * QB
    batch = passages.reshape(N_COL * PPD, D)
    hard = hard_passages.reshape(N_COL * HR, D)
    qgroups = queries.reshape(N_ROW, rows_per, D)
    pgroups = positives.reshape(N_ROW, rows_per)
    hgroups = hard_blocks.reshape(N_ROW, QBD, KH)
    block_of = jnp.arange(N_COL * HR, dtype=jnp.int32) // HR
    every_block = jnp.arange(N_COL, dtype=jnp.int32)
    flat_index = jnp.arange(N_COL * PPD, dtype=jnp.int32)

    def group(carry, item):
        rows, posit, chosen_ids = item
        scores = lax.dot_general(rows, batch, (((1,), (1,)), ((), ())), preferred_element_type=jnp.float32) * scale
        hard_scores = lax.dot_general(rows, hard, (((1,), (1,)), ((), ())), preferred_element_type=jnp.float32) * scale
        chosen = jnp.any(chosen_ids[:, :, None] == every_block[None, None, :], axis=1)
        live = jnp.repeat(chosen[:, block_of], QB, axis=0)
        hard_scores = jnp.where(live, hard_scores, -jnp.inf)
        top = jnp.maximum(jnp.max(scores, axis=1), jnp.max(hard_scores, axis=1))
        total = jnp.sum(jnp.exp(scores - top[:, None]), axis=1) + jnp.sum(jnp.exp(hard_scores - top[:, None]), axis=1)
        lse = top + jnp.log(total)
        onehot = (flat_index[None, :] == posit[:, None]).astype(jnp.float32)
        pos_score = jnp.sum(onehot * scores, axis=1)
        losses = lse - pos_score
        weights = (jnp.exp(scores - lse[:, None]) - onehot).astype(jnp.bfloat16)
        hard_weights = jnp.exp(hard_scores - lse[:, None]).astype(jnp.bfloat16)
        part = lax.dot_general(weights, rows, (((0,), (0,)), ((), ())), preferred_element_type=jnp.float32).astype(jnp.bfloat16)
        hard_part = lax.dot_general(hard_weights, rows, (((0,), (0,)), ((), ())), preferred_element_type=jnp.float32).astype(jnp.bfloat16)
        part = lax.optimization_barrier(part).astype(jnp.float32)
        hard_part = lax.optimization_barrier(hard_part).astype(jnp.float32)
        return (carry[0] + part, carry[1] + hard_part), losses

    start = (jnp.zeros((N_COL * PPD, D), jnp.float32), jnp.zeros((N_COL * HR, D), jnp.float32))
    sums, losses = lax.scan(group, start, (qgroups, pgroups, hgroups))
    passage_grads = sums[0].reshape(N_COL, PPD, D).astype(jnp.bfloat16)
    hard_grads = sums[1].reshape(N_COL, HR, D).astype(jnp.bfloat16)
    return (losses.reshape(N_ROW * rows_per), passage_grads, hard_grads)
```

```python
import jax
import jax.numpy as jnp
from jax import lax
from jax.sharding import PartitionSpec as P

F32 = jnp.float32
BF16 = jnp.bfloat16
SIDE = 4
Z_GROUPS = [[x * SIDE + z for z in range(SIDE)] for x in range(SIDE)]
X_GROUPS = [[x * SIDE + z for x in range(SIDE)] for z in range(SIDE)]


def swap(array, axis, groups=None):
    return lax.all_to_all(array, axis, 0, 0, tiled=True, axis_index_groups=groups)


def gather(rows, groups):
    copies = jnp.broadcast_to(rows[None], (SIDE,) + rows.shape)
    return swap(copies, "row", groups).reshape((-1,) + rows.shape[1:])


def scatter_sum(rows, groups):
    got = swap(rows.reshape((SIDE, -1) + rows.shape[1:]), "row", groups)
    return jnp.sum(got.astype(F32), axis=0).astype(BF16)


def on_device(queries, positives, hard_blocks, passages, hard_passages):
    count, depth = queries.shape
    scale = depth ** (-0.5)
    column = lax.axis_index("col")
    n_col = lax.axis_size("col")
    n_row = lax.axis_size("row")
    batch_part, hard_part = passages.shape[1], hard_passages.shape[1]
    part = batch_part + hard_part
    own = jnp.concatenate([passages, hard_passages], axis=1)
    moved = swap(own.reshape(n_col, -1), "col")
    moved = moved.reshape(n_col, part, -1).transpose(1, 0, 2).reshape(part, depth)
    keys = lax.all_gather(moved, "row", axis_index_groups=Z_GROUPS, tiled=True)
    keys = gather(keys, X_GROUPS)
    slots = n_row * part
    scores = lax.dot_general(keys, queries, (((1,), (1,)), ((), ())), preferred_element_type=F32)
    scores = scores * scale
    slot = lax.broadcasted_iota(jnp.int32, (slots, 1), 0)
    is_hard = slot % part >= batch_part
    flat = column * (n_row * batch_part) + (slot // part) * batch_part + slot % part
    onehot = jnp.logical_and(jnp.logical_not(is_hard), flat == positives[None, :])
    chosen = jnp.any(hard_blocks == column, axis=1)
    live = jnp.repeat(chosen, count // hard_blocks.shape[0])[None, :]
    kept = jnp.logical_or(jnp.logical_not(is_hard), live)
    scores = jnp.where(kept, scores, -jnp.inf)
    top = jnp.max(scores, axis=0)
    total = jnp.sum(jnp.exp(scores - top[None, :]), axis=0)
    pos = jnp.sum(jnp.where(onehot, scores, 0.0), axis=0)
    stats = jnp.stack([top + jnp.log(total), pos])
    stats = swap(jnp.broadcast_to(stats[None], (n_col,) + stats.shape), "col")
    parts = stats[:, 0]
    all_top = jnp.max(parts, axis=0)
    lse = all_top + jnp.log(jnp.sum(jnp.exp(parts - all_top[None]), axis=0))
    losses = lse - jnp.sum(stats[:, 1], axis=0)
    weights = (jnp.exp(scores - lse[None, :]) - onehot.astype(F32)).astype(BF16)
    grads = lax.dot_general(weights, queries, (((1,), (0,)), ((), ())), preferred_element_type=F32)
    grads = scatter_sum(scatter_sum(grads.astype(BF16), X_GROUPS), Z_GROUPS)
    return (losses, grads[None, :batch_part], grads[None, batch_part:])


def solution(mesh):
    in_specs = (
        P("row", None),
        P("row"),
        P("row", None),
        P(None, "row", "col"),
        P(None, "row", "col"),
    )
    out_specs = (P("row"), P("col", "row", None), P("col", "row", None))
    return jax.shard_map(
        on_device, mesh=mesh, in_specs=in_specs, out_specs=out_specs, check_vma=False
    )
```

```python
import jax
import jax.numpy as jnp
from jax import lax
from jax.sharding import PartitionSpec as P

F32 = jnp.float32
BF16 = jnp.bfloat16
LANES = 128
SIDE = 4
Z_GROUPS = [[x * SIDE + z for z in range(SIDE)] for x in range(SIDE)]
X_GROUPS = [[x * SIDE + z for x in range(SIDE)] for z in range(SIDE)]


def swap(array, axis, groups=None):
    return lax.all_to_all(array, axis, 0, 0, tiled=True, axis_index_groups=groups)


def to_tiles(rows, height):
    count, depth = rows.shape
    tiles = rows.reshape(count // height, height, depth // LANES, LANES).transpose(0, 2, 1, 3)
    return tiles.reshape(count // height, -1, LANES)


def from_tiles(tiles, height):
    count, size, _ = tiles.shape
    rows = tiles.reshape(count, size // height, height, LANES).transpose(0, 2, 1, 3)
    return rows.reshape(count * height, -1)


def fold(rows):
    half = rows.shape[1] // 2
    return jnp.concatenate([rows[:, :half], rows[:, half:]], axis=2)


def unfold(rows):
    half = rows.shape[2] // 2
    pairs = rows.reshape(rows.shape[0] // 2, 2, rows.shape[1], rows.shape[2])
    return jnp.concatenate(
        [
            jnp.concatenate([pairs[:, 0, :, part], pairs[:, 1, :, part]], axis=2)
            for part in (slice(0, half), slice(half, None))
        ],
        axis=1,
    ).reshape(-1, LANES)


def on_device(queries, positives, hard_blocks, passages, hard_passages):
    count, depth = queries.shape
    scale = depth ** (-0.5)
    column = lax.axis_index("col")
    n_col = lax.axis_size("col")
    rows, hard_rows = passages.shape[1], hard_passages.shape[1]
    part = rows + hard_rows
    period, batch_rows = SIDE * part, SIDE * rows

    own = jnp.concatenate([fold(passages), fold(hard_passages)], axis=1)
    moved = swap(own, "col")
    cut = rows * depth // LANES
    sent = jnp.concatenate([unfold(moved[:, : rows // 2]), unfold(moved[:, rows // 2 :])])
    gathered = lax.all_gather(sent, "row", axis_index_groups=Z_GROUPS, tiled=True)
    gathered = jnp.broadcast_to(gathered[None], (SIDE,) + gathered.shape)
    gathered = swap(gathered, "row", X_GROUPS).reshape(SIDE, SIDE, -1, LANES)
    batch = gathered[:, :, :cut].reshape(SIDE * SIDE, cut, LANES)
    hard = gathered[:, :, cut:].reshape(SIDE * SIDE, -1, LANES)
    batch = from_tiles(batch, rows).reshape(SIDE, batch_rows, depth)
    hard = from_tiles(hard, hard_rows).reshape(SIDE, -1, depth)
    keys = jnp.concatenate([batch, hard], axis=1).reshape(-1, depth)

    block_rows = keys.shape[0] // period * batch_rows
    within = positives % block_rows
    target = within // batch_rows * period + within % batch_rows
    target = jnp.where(positives // block_rows == column, target, -1)[None, :]
    chosen = jnp.any(hard_blocks == column, axis=1)
    live = jnp.repeat(chosen, count // hard_blocks.shape[0])[None, :]
    scores = lax.dot_general(keys, queries, (((1,), (1,)), ((), ())), preferred_element_type=F32)
    slot = lax.broadcasted_iota(jnp.int32, scores.shape, 0)
    kept = jnp.logical_or(slot % period < batch_rows, live)
    scores = jnp.where(kept, scores * scale, -jnp.inf)
    top = jnp.max(scores, axis=0)
    total = jnp.sum(jnp.exp(scores - top[None, :]), axis=0)
    pos = jnp.sum(jnp.where(slot == target, scores, 0.0), axis=0)
    stats = jnp.stack([top + jnp.log(total), pos])

    other = lax.ppermute(stats, "col", [(i, i ^ 1) for i in range(n_col)])
    high = jnp.maximum(stats[0], other[0])
    low = jnp.minimum(stats[0], other[0])
    joined = jnp.stack([high + jnp.log1p(jnp.exp(low - high)), stats[1] + other[1]])
    cores = [list(range(core, n_col, 2)) for core in range(2)]
    parts = swap(jnp.broadcast_to(joined[None], (n_col // 2,) + joined.shape), "col", cores)
    tops = parts[:, 0]
    all_top = jnp.max(tops, axis=0)
    lse = all_top + jnp.log(jnp.sum(jnp.exp(tops - all_top[None]), axis=0))
    losses = lse - jnp.sum(parts[:, 1], axis=0)

    slot = lax.broadcasted_iota(jnp.int32, scores.shape, 0)
    weights = (jnp.exp(scores - lse[None, :]) - (slot == target).astype(F32)).astype(BF16)
    grads = lax.dot_general(weights, queries, (((1,), (0,)), ((), ())), preferred_element_type=F32)
    grads = to_tiles(grads.astype(BF16), rows).reshape(SIDE, -1, LANES)
    got = swap(grads, "row", X_GROUPS)
    total = jnp.sum(got.astype(F32), axis=0).astype(BF16)
    batch = total[: SIDE * cut].reshape(SIDE, cut, LANES)
    hard = from_tiles(total[SIDE * cut :].reshape(-1, cut, LANES), rows)
    hard = to_tiles(hard, hard_rows)
    got = swap(jnp.concatenate([batch, hard], axis=1), "row", Z_GROUPS)
    total = jnp.sum(got.astype(F32), axis=0).astype(BF16)[None]
    return (
        losses,
        from_tiles(total[:, :cut], rows)[None],
        from_tiles(total[:, cut:], hard_rows)[None],
    )


def solution(mesh):
    in_specs = (
        P("row", None),
        P("row"),
        P("row", None),
        P(None, "row", "col"),
        P(None, "row", "col"),
    )
    out_specs = (P("row"), P("col", "row", None), P("col", "row", None))
    return jax.shard_map(
        on_device, mesh=mesh, in_specs=in_specs, out_specs=out_specs, check_vma=False
    )
```

```python
import jax
import jax.numpy as jnp
from jax import lax
from jax.sharding import PartitionSpec as P

F32 = jnp.float32
BF16 = jnp.bfloat16
LANES = 128
SIDE = 4
Z_GROUPS = [[x * SIDE + z for z in range(SIDE)] for x in range(SIDE)]


def swap(array, axis, groups=None):
    return lax.all_to_all(array, axis, 0, 0, tiled=True, axis_index_groups=groups)


def shift(step):
    size = SIDE * SIDE
    return [(i, (i + step * SIDE) % size) for i in range(size)]


def to_tiles(rows, height):
    count, depth = rows.shape
    tiles = rows.reshape(count // height, height, depth // LANES, LANES).transpose(0, 2, 1, 3)
    return tiles.reshape(count // height, -1, LANES)


def from_tiles(tiles, height):
    count, size, _ = tiles.shape
    rows = tiles.reshape(count, size // height, height, LANES).transpose(0, 2, 1, 3)
    return rows.reshape(count * height, -1)


def fold(rows):
    half = rows.shape[1] // 2
    return jnp.concatenate([rows[:, :half], rows[:, half:]], axis=2)


def unfold(rows):
    half = rows.shape[2] // 2
    pairs = rows.reshape(rows.shape[0] // 2, 2, rows.shape[1], rows.shape[2])
    return jnp.concatenate(
        [
            jnp.concatenate([pairs[:, 0, :, part], pairs[:, 1, :, part]], axis=2)
            for part in (slice(0, half), slice(half, None))
        ],
        axis=1,
    ).reshape(-1, LANES)


def on_device(queries, positives, hard_blocks, passages, hard_passages):
    count, depth = queries.shape
    scale = depth ** (-0.5)
    column = lax.axis_index("col")
    n_col = lax.axis_size("col")
    rows, hard_rows = passages.shape[1], hard_passages.shape[1]
    part = rows + hard_rows
    period, batch_rows = SIDE * part, SIDE * rows

    own = jnp.concatenate([fold(passages), fold(hard_passages)], axis=1)
    moved = swap(own, "col")
    cut = rows * depth // LANES
    sent = jnp.concatenate([unfold(moved[:, : rows // 2]), unfold(moved[:, rows // 2 :])])
    gathered = lax.all_gather(sent, "row", axis_index_groups=Z_GROUPS, tiled=True)
    shares = [gathered] + [lax.ppermute(gathered, "row", shift(step)) for step in range(1, SIDE)]

    plane = lax.axis_index("row") // SIDE
    block_rows = lax.axis_size("row") * rows
    within = positives % block_rows
    target = (plane - within // batch_rows) % SIDE * period + within % batch_rows
    target = jnp.where(positives // block_rows == column, target, -1)[None, :]
    chosen = jnp.any(hard_blocks == column, axis=1)
    live = jnp.repeat(chosen, count // hard_blocks.shape[0])[None, :]

    def score(tiles, first):
        tiles = jnp.stack(tiles).reshape(-1, sent.shape[0], LANES)
        batch = from_tiles(tiles[:, :cut], rows).reshape(-1, batch_rows, depth)
        hard = from_tiles(tiles[:, cut:], hard_rows).reshape(-1, period - batch_rows, depth)
        keys = jnp.concatenate([batch, hard], axis=1).reshape(-1, depth)
        s = lax.dot_general(keys, queries, (((1,), (1,)), ((), ())), preferred_element_type=F32)
        slot = lax.broadcasted_iota(jnp.int32, s.shape, 0) + first
        kept = jnp.logical_or(slot % period < batch_rows, live)
        return jnp.where(kept, s * scale, -jnp.inf)

    scores = (score(shares[:1], 0), score(shares[1:], period))
    top = jnp.maximum(jnp.max(scores[0], axis=0), jnp.max(scores[1], axis=0))
    scores = jnp.concatenate(scores)
    slot = lax.broadcasted_iota(jnp.int32, scores.shape, 0)
    total = jnp.sum(jnp.exp(scores - top[None, :]), axis=0)
    pos = jnp.sum(jnp.where(slot == target, scores, 0.0), axis=0)
    stats = jnp.stack([top + jnp.log(total), pos])

    other = lax.ppermute(stats, "col", [(i, i ^ 1) for i in range(n_col)])
    high = jnp.maximum(stats[0], other[0])
    low = jnp.minimum(stats[0], other[0])
    joined = jnp.stack([high + jnp.log1p(jnp.exp(low - high)), stats[1] + other[1]])
    cores = [list(range(core, n_col, 2)) for core in range(2)]
    parts = swap(jnp.broadcast_to(joined[None], (n_col // 2,) + joined.shape), "col", cores)
    tops = parts[:, 0]
    all_top = jnp.max(tops, axis=0)
    lse = all_top + jnp.log(jnp.sum(jnp.exp(tops - all_top[None]), axis=0))
    losses = lse - jnp.sum(parts[:, 1], axis=0)

    weights = (jnp.exp(scores - lse[None, :]) - (slot == target).astype(F32)).astype(BF16)
    grads = lax.dot_general(weights, queries, (((1,), (0,)), ((), ())), preferred_element_type=F32)
    grads = to_tiles(grads.astype(BF16), rows).reshape(SIDE, -1, LANES)
    total = grads[0].astype(F32)
    for step in range(1, SIDE):
        total = total + lax.ppermute(grads[step], "row", shift(-step)).astype(F32)
    total = total.astype(BF16)
    batch = total[: SIDE * cut].reshape(SIDE, cut, LANES)
    hard = from_tiles(total[SIDE * cut :].reshape(-1, cut, LANES), rows)
    hard = to_tiles(hard, hard_rows)
    got = swap(jnp.concatenate([batch, hard], axis=1), "row", Z_GROUPS)
    total = jnp.sum(got.astype(F32), axis=0).astype(BF16)[None]
    return (
        losses,
        from_tiles(total[:, :cut], rows)[None],
        from_tiles(total[:, cut:], hard_rows)[None],
    )


def solution(mesh):
    in_specs = (
        P("row", None),
        P("row"),
        P("row", None),
        P(None, "row", "col"),
        P(None, "row", "col"),
    )
    out_specs = (P("row"), P("col", "row", None), P("col", "row", None))
    return jax.shard_map(
        on_device, mesh=mesh, in_specs=in_specs, out_specs=out_specs, check_vma=False
    )
```

```python
import functools

import jax
import jax.numpy as jnp
from jax import lax
from jax.experimental import pallas as pl
from jax.experimental.pallas import tpu as pltpu
from jax.sharding import PartitionSpec as P

F32 = jnp.float32
BF16 = jnp.bfloat16
LANES = 128
SIDE = 4
Z_GROUPS = [[x * SIDE + z for z in range(SIDE)] for x in range(SIDE)]
X_GROUPS = [[x * SIDE + z for x in range(SIDE)] for z in range(SIDE)]


def swap(array, axis, groups=None):
    return lax.all_to_all(array, axis, 0, 0, tiled=True, axis_index_groups=groups)


def to_tiles(rows, height):
    count, depth = rows.shape
    tiles = rows.reshape(count // height, height, depth // LANES, LANES).transpose(0, 2, 1, 3)
    return tiles.reshape(count // height, -1, LANES)


def from_tiles(tiles, height):
    count, size, _ = tiles.shape
    rows = tiles.reshape(count, size // height, height, LANES).transpose(0, 2, 1, 3)
    return rows.reshape(count * height, -1)


def score_kernel(
    period, batch_rows, scale, column, hard_blocks, keys, queries, positives, scores, stats, target,
    held, arrived,
):
    slots, count = scores.shape
    blocks, picks = hard_blocks.shape
    block_rows = slots // period * batch_rows
    steps, ahead = arrived.shape[0], 2
    size = count // steps

    def fetch(step):
        part = pl.ds(pl.multiple_of(step * size, size), size)
        return pltpu.make_async_copy(queries.at[part], held.at[part], arrived.at[step])

    for step in range(ahead):
        fetch(step).start()

    @pl.loop(0, steps)
    def _(step):
        fetch(step).wait()

        @pl.when(step + ahead < steps)
        def _():
            fetch(step + ahead).start()

        part = pl.ds(pl.multiple_of(step * size, size), size)
        s = lax.dot_general(
            keys[...], held[part, :], (((1,), (1,)), ((), ())), preferred_element_type=F32
        )
        query = lax.broadcasted_iota(jnp.int32, (1, size), 1) + step * size
        query = query // (count // blocks)
        live = query < 0
        for block in range(blocks):
            hit = hard_blocks[block, 0] == column[0]
            for pick in range(1, picks):
                hit = jnp.logical_or(hit, hard_blocks[block, pick] == column[0])
            live = jnp.logical_or(live, query == jnp.where(hit, block, -1))
        place = positives[:, part]
        within = place % block_rows
        own = within // batch_rows * period + within % batch_rows
        own = jnp.where(place // block_rows == column[0], own, -1)
        slot = lax.broadcasted_iota(jnp.int32, s.shape, 0)
        s = jnp.where(jnp.logical_or(slot % period < batch_rows, live), s * scale, -jnp.inf)
        top = jnp.max(s, axis=0, keepdims=True)
        total = jnp.sum(jnp.exp(s - top), axis=0, keepdims=True)
        scores[:, part] = s
        stats[0:1, part] = top + jnp.log(total)
        stats[1:2, part] = jnp.sum(jnp.where(slot == own, s, 0.0), axis=0, keepdims=True)
        target[:, part] = own


def score(column, hard_blocks, keys, queries, positives, period, batch_rows, scale):
    slots, depth = keys.shape
    count = queries.shape[0]
    scalars = pl.BlockSpec(memory_space=pltpu.SMEM)
    whole = pl.BlockSpec(memory_space=pltpu.VMEM)
    return pl.pallas_call(
        functools.partial(score_kernel, period, batch_rows, scale),
        in_specs=[scalars, scalars, whole, pl.BlockSpec(memory_space=pl.ANY), whole],
        out_specs=[whole] * 3,
        out_shape=[
            jax.ShapeDtypeStruct((slots, count), F32),
            jax.ShapeDtypeStruct((2, count), F32),
            jax.ShapeDtypeStruct((1, count), jnp.int32),
        ],
        scratch_shapes=[pltpu.VMEM(queries.shape, queries.dtype), pltpu.SemaphoreType.DMA((4,))],
        compiler_params=pltpu.CompilerParams(vmem_limit_bytes=50 * 1024 * 1024),
        cost_estimate=pl.CostEstimate(
            flops=2 * slots * depth * count,
            bytes_accessed=2 * depth * (slots + count) + 4 * slots * count,
            transcendentals=slots * count,
        ),
    )(column, hard_blocks, keys, queries, positives)


def fold(rows):
    half = rows.shape[1] // 2
    return jnp.concatenate([rows[:, :half], rows[:, half:]], axis=2)


def unfold(rows):
    half = rows.shape[2] // 2
    pairs = rows.reshape(rows.shape[0] // 2, 2, rows.shape[1], rows.shape[2])
    return jnp.concatenate(
        [
            jnp.concatenate([pairs[:, 0, :, part], pairs[:, 1, :, part]], axis=2)
            for part in (slice(0, half), slice(half, None))
        ],
        axis=1,
    )


def on_device(queries, positives, hard_blocks, passages, hard_passages):
    count, depth = queries.shape
    scale = depth ** (-0.5)
    column = lax.axis_index("col")
    n_col = lax.axis_size("col")
    rows, hard_rows = passages.shape[1], hard_passages.shape[1]
    part = rows + hard_rows
    period, batch_rows = SIDE * part, SIDE * rows

    own = fold(jnp.concatenate([passages, hard_passages], axis=1))
    moved = unfold(swap(own, "col"))
    cut = rows * depth // LANES
    sent = jnp.concatenate([a.reshape(-1, LANES) for a in (moved[:, :rows], moved[:, rows:])])
    gathered = lax.all_gather(sent, "row", axis_index_groups=Z_GROUPS, tiled=True)
    gathered = jnp.broadcast_to(gathered[None], (SIDE,) + gathered.shape)
    gathered = swap(gathered, "row", X_GROUPS).reshape(SIDE, SIDE, -1, LANES)
    batch = gathered[:, :, :cut].reshape(SIDE * SIDE, cut, LANES)
    hard = gathered[:, :, cut:].reshape(SIDE * SIDE, -1, LANES)
    batch = from_tiles(batch, rows).reshape(SIDE, batch_rows, depth)
    hard = from_tiles(hard, hard_rows).reshape(SIDE, -1, depth)
    keys = jnp.concatenate([batch, hard], axis=1).reshape(-1, depth)

    scores, stats, target = score(
        column[None], hard_blocks, keys, queries, positives[None, :], period, batch_rows, scale
    )

    other = lax.ppermute(stats, "col", [(i, i ^ 1) for i in range(n_col)])
    high = jnp.maximum(stats[0], other[0])
    low = jnp.minimum(stats[0], other[0])
    joined = jnp.stack([high + jnp.log1p(jnp.exp(low - high)), stats[1] + other[1]])
    cores = [list(range(core, n_col, 2)) for core in range(2)]
    parts = swap(jnp.broadcast_to(joined[None], (n_col // 2,) + joined.shape), "col", cores)
    tops = parts[:, 0]
    all_top = jnp.max(tops, axis=0)
    lse = all_top + jnp.log(jnp.sum(jnp.exp(tops - all_top[None]), axis=0))
    losses = lse - jnp.sum(parts[:, 1], axis=0)

    slot = lax.broadcasted_iota(jnp.int32, scores.shape, 0)
    weights = (jnp.exp(scores - lse[None, :]) - (slot == target).astype(F32)).astype(BF16)
    grads = lax.dot_general(weights, queries, (((1,), (0,)), ((), ())), preferred_element_type=F32)
    grads = to_tiles(grads.astype(BF16), rows).reshape(SIDE, -1, LANES)
    got = swap(grads, "row", X_GROUPS)
    total = jnp.sum(got.astype(F32), axis=0).astype(BF16)
    batch = total[: SIDE * cut].reshape(SIDE, cut, LANES)
    hard = from_tiles(total[SIDE * cut :].reshape(-1, cut, LANES), rows)
    hard = to_tiles(hard, hard_rows)
    got = swap(jnp.concatenate([batch, hard], axis=1), "row", Z_GROUPS)
    total = jnp.sum(got.astype(F32), axis=0).astype(BF16)[None]
    return (
        losses,
        from_tiles(total[:, :cut], rows)[None],
        from_tiles(total[:, cut:], hard_rows)[None],
    )


def solution(mesh):
    in_specs = (
        P("row", None),
        P("row"),
        P("row", None),
        P(None, "row", "col"),
        P(None, "row", "col"),
    )
    out_specs = (P("row"), P("col", "row", None), P("col", "row", None))
    return jax.shard_map(
        on_device, mesh=mesh, in_specs=in_specs, out_specs=out_specs, check_vma=False
    )
```

```python
import jax
import jax.numpy as jnp
from jax import lax
from jax.experimental import pallas as pl
from jax.experimental.pallas import tpu as pltpu
from jax.sharding import PartitionSpec as P

F32 = jnp.float32
BF16 = jnp.bfloat16
LANES = 128
SIDE = 4
Z_GROUPS = [[x * SIDE + z for z in range(SIDE)] for x in range(SIDE)]
X_GROUPS = [[x * SIDE + z for x in range(SIDE)] for z in range(SIDE)]


def swap(array, axis, groups=None):
    return lax.all_to_all(array, axis, 0, 0, tiled=True, axis_index_groups=groups)


def to_tiles(rows, height):
    count, depth = rows.shape
    tiles = rows.reshape(count // height, height, depth // LANES, LANES).transpose(0, 2, 1, 3)
    return tiles.reshape(count // height, -1, LANES)


def from_tiles(tiles, height):
    count, size, _ = tiles.shape
    rows = tiles.reshape(count, size // height, height, LANES).transpose(0, 2, 1, 3)
    return rows.reshape(count * height, -1)


def finish_kernel(parts, batch, hard):
    total = parts[0].astype(F32)
    for part in range(1, parts.shape[0]):
        total = total + parts[part].astype(F32)
    cut = batch.shape[0]
    batch[...] = total[:cut].astype(batch.dtype)
    hard[...] = total[cut:].astype(hard.dtype)


def finish(parts, cut):
    shapes = [(cut, LANES), (parts.shape[1] - cut, LANES)]
    return pl.pallas_call(
        finish_kernel,
        grid=(1,),
        in_specs=[pl.BlockSpec(parts.shape, lambda i: (0, 0, 0))],
        out_specs=[pl.BlockSpec(shape, lambda i: (0, 0)) for shape in shapes],
        out_shape=[jax.ShapeDtypeStruct(shape, parts.dtype) for shape in shapes],
        compiler_params=pltpu.CompilerParams(vmem_limit_bytes=16 * 1024 * 1024),
    )(parts)


def fold(rows):
    half = rows.shape[1] // 2
    return jnp.concatenate([rows[:, :half], rows[:, half:]], axis=2)


def unfold(rows):
    half = rows.shape[2] // 2
    pairs = rows.reshape(rows.shape[0] // 2, 2, rows.shape[1], rows.shape[2])
    return jnp.concatenate(
        [
            jnp.concatenate([pairs[:, 0, :, part], pairs[:, 1, :, part]], axis=2)
            for part in (slice(0, half), slice(half, None))
        ],
        axis=1,
    )


def on_device(queries, positives, hard_blocks, passages, hard_passages):
    count, depth = queries.shape
    scale = depth ** (-0.5)
    column = lax.axis_index("col")
    n_col = lax.axis_size("col")
    rows, hard_rows = passages.shape[1], hard_passages.shape[1]
    part = rows + hard_rows
    period, batch_rows = SIDE * part, SIDE * rows

    own = fold(jnp.concatenate([passages, hard_passages], axis=1))
    moved = unfold(swap(own, "col"))
    cut = rows * depth // LANES
    sent = jnp.concatenate([a.reshape(-1, LANES) for a in (moved[:, :rows], moved[:, rows:])])
    gathered = lax.all_gather(sent, "row", axis_index_groups=Z_GROUPS, tiled=True)
    gathered = jnp.broadcast_to(gathered[None], (SIDE,) + gathered.shape)
    gathered = swap(gathered, "row", X_GROUPS).reshape(SIDE, SIDE, -1, LANES)
    batch = gathered[:, :, :cut].reshape(SIDE * SIDE, cut, LANES)
    hard = gathered[:, :, cut:].reshape(SIDE * SIDE, -1, LANES)
    batch = from_tiles(batch, rows).reshape(SIDE, batch_rows, depth)
    hard = from_tiles(hard, hard_rows).reshape(SIDE, -1, depth)
    keys = jnp.concatenate([batch, hard], axis=1).reshape(-1, depth)

    block_rows = keys.shape[0] // period * batch_rows
    within = positives % block_rows
    target = within // batch_rows * period + within % batch_rows
    target = jnp.where(positives // block_rows == column, target, -1)[None, :]
    chosen = jnp.any(hard_blocks == column, axis=1)
    live = jnp.repeat(chosen, count // hard_blocks.shape[0])[None, :]
    scores = lax.dot_general(keys, queries, (((1,), (1,)), ((), ())), preferred_element_type=F32)
    slot = lax.broadcasted_iota(jnp.int32, scores.shape, 0)
    kept = jnp.logical_or(slot % period < batch_rows, live)
    scores = jnp.where(kept, scores * scale, -jnp.inf)
    top = jnp.max(scores, axis=0)
    total = jnp.sum(jnp.exp(scores - top[None, :]), axis=0)
    pos = jnp.sum(jnp.where(slot == target, scores, 0.0), axis=0)
    stats = jnp.stack([top + jnp.log(total), pos])

    other = lax.ppermute(stats, "col", [(i, i ^ 1) for i in range(n_col)])
    high = jnp.maximum(stats[0], other[0])
    low = jnp.minimum(stats[0], other[0])
    joined = jnp.stack([high + jnp.log1p(jnp.exp(low - high)), stats[1] + other[1]])
    cores = [list(range(core, n_col, 2)) for core in range(2)]
    parts = swap(jnp.broadcast_to(joined[None], (n_col // 2,) + joined.shape), "col", cores)
    tops = parts[:, 0]
    all_top = jnp.max(tops, axis=0)
    lse = all_top + jnp.log(jnp.sum(jnp.exp(tops - all_top[None]), axis=0))
    losses = lse - jnp.sum(parts[:, 1], axis=0)

    slot = lax.broadcasted_iota(jnp.int32, scores.shape, 0)
    weights = (jnp.exp(scores - lse[None, :]) - (slot == target).astype(F32)).astype(BF16)
    grads = lax.dot_general(weights, queries, (((1,), (0,)), ((), ())), preferred_element_type=F32)
    grads = to_tiles(grads.astype(BF16), rows).reshape(SIDE, -1, LANES)
    got = swap(grads, "row", X_GROUPS)
    total = jnp.sum(got.astype(F32), axis=0).astype(BF16)
    batch = total[: SIDE * cut].reshape(SIDE, cut, LANES)
    hard = from_tiles(total[SIDE * cut :].reshape(-1, cut, LANES), rows)
    hard = to_tiles(hard, hard_rows)
    got = swap(jnp.concatenate([batch, hard], axis=1), "row", Z_GROUPS)
    batch, hard = finish(got, cut)
    return (losses, from_tiles(batch[None], rows)[None], from_tiles(hard[None], hard_rows)[None])


def solution(mesh):
    in_specs = (
        P("row", None),
        P("row"),
        P("row", None),
        P(None, "row", "col"),
        P(None, "row", "col"),
    )
    out_specs = (P("row"), P("col", "row", None), P("col", "row", None))
    return jax.shard_map(
        on_device, mesh=mesh, in_specs=in_specs, out_specs=out_specs, check_vma=False
    )
```
